512 devices in a mesh: row: 32 (over y, x, core), col: 16 (over z).
Axes of the slice: x: 4, y: 4, z: 16, core: 2. Of those that a mesh axis runs over, the one named last changes fastest.
Arguments:
- activations: bfloat16 [512, 12288], P('col', 'row'), may hold values from -6 to 6
- up_weight: bfloat16 [12288, 24576], P('row', 'col'), may hold values from -0.0546875 to 0.0546875
- down_weight: bfloat16 [24576, 12288], P('col', 'row'), may hold values from -0.0390625 to 0.0390625
- cotangent: bfloat16 [512, 12288], P('col', 'row'), may hold values from -6 to 6
Outputs:
- output: bfloat16 [512, 12288], P('col', 'row')
- grad_input: bfloat16 [512, 12288], P('col', 'row')
- grad_up: bfloat16 [12288, 24576], P('row', 'col')
- grad_down: bfloat16 [24576, 12288], P('col', 'row')
The draws below stay inside these ranges and needn't reach their ends.
All inputs are finite; a program needn't handle non-finite values.
Results may differ from the reference program's by a relative error of at most 0.034.
Values may be sent and summed in bfloat16 or wider, within the bound.
No kernel may reach another device: no remote copies, remote signals or barrier semaphores. Data moves between devices by JAX's collectives and lax.ppermute only.
A program may use at most 64 MiB of HBM per device.

```python
import math
import jax
import jax.numpy as jnp
from jax import lax

D = 12288
FF = 24576
TOKENS = 512
N_ROW = 32
N_COL = 16


def level_of(own_key, shape, shards, least, top_value):
    level = 1.0
    for dim, parts in shards:
        draws = jax.random.uniform(jax.random.fold_in(jax.random.fold_in(own_key, 6), dim), (parts,), jnp.float32, least / len(shards), top_value / len(shards))
        level = level * jnp.repeat(jnp.exp(draws), shape[dim] // parts).reshape((-1,) + (1,) * (len(shape) - 1 - dim))
    return level


def bell_draw(key, dims, scale, reach, shards=(), held_as=jnp.bfloat16):
    loudness = level_of(key, dims, shards, -0.22, 0.18) if shards else 1.0
    result = jax.random.normal(key, dims, jnp.float32) * scale * loudness
    return jnp.minimum(jnp.maximum(result, -reach), reach).astype(held_as)


def setup_inputs(seed: int = 0) -> dict:
    arg_keys = jax.random.split(jax.random.key(seed), 5)
    return {
        "activations": bell_draw(arg_keys[0], (TOKENS, D), 1.0, 6.0, ((0, 16), (1, 32))),
        "up_weight": bell_draw(arg_keys[1], (D, FF), D ** -0.5, 0.0546875, ((0, 32), (1, 16))),
        "down_weight": bell_draw(arg_keys[2], (FF, D), FF ** -0.5, 0.0390625, ((0, 16), (1, 32))),
        "cotangent": bell_draw(arg_keys[3], (TOKENS, D), 1.0, 6.0, ((0, 16), (1, 32))),
    }


def gelu_tanh(z):
    c = math.sqrt(2.0 / math.pi)
    return 0.5 * z * (1.0 + jnp.tanh(c * (z + 0.044715 * z * z * z)))

def gelu_slope(z):
    c = math.sqrt(2.0 / math.pi)
    t = jnp.tanh(c * (z + 0.044715 * z * z * z))
    return 0.5 * (1.0 + t) + 0.5 * z * (1.0 - t * t) * c * (1.0 + 3.0 * 0.044715 * z * z)

def blocked_sum(left, right, blocks, right_axis):
    width = left.shape[1] // blocks
    count = left.shape[0]
    outer = right.shape[1 - right_axis]

    def add_block(index, total):
        begin = (index * width).astype(jnp.int32)
        piece = lax.dynamic_slice_in_dim(left, begin, width, 1)
        other = lax.dynamic_slice_in_dim(right, begin, width, right_axis)
        if right_axis == 0:
            partial_sum = jnp.dot(piece, other, preferred_element_type=jnp.float32)
        else:
            partial_sum = jnp.dot(piece, other.T, preferred_element_type=jnp.float32)
        rounded = lax.optimization_barrier(partial_sum.astype(jnp.bfloat16))
        return total + rounded.astype(jnp.float32)
    start_total = jnp.zeros((count, outer), jnp.float32)
    return lax.fori_loop(0, blocks, add_block, start_total)

def reference(activations, up_weight, down_weight, cotangent):
    pre_act = blocked_sum(activations, up_weight, N_ROW, 0)
    hidden = gelu_tanh(pre_act).astype(jnp.bfloat16)
    output = blocked_sum(hidden, down_weight, N_COL, 0).astype(jnp.bfloat16)
    grad_hidden = blocked_sum(cotangent, down_weight, N_ROW, 1)
    slope = (grad_hidden * gelu_slope(pre_act)).astype(jnp.bfloat16)
    grad_down = jnp.dot(hidden.T, cotangent, preferred_element_type=jnp.float32).astype(jnp.bfloat16)
    grad_up = jnp.dot(activations.T, slope, preferred_element_type=jnp.float32).astype(jnp.bfloat16)
    grad_input = blocked_sum(slope, up_weight, N_COL, 1).astype(jnp.bfloat16)
    return (output, grad_input, grad_up, grad_down)
```

```python
import math

import jax
import jax.numpy as jnp
from jax import lax
from jax.sharding import Mesh
from jax.sharding import PartitionSpec as P

BF16 = jnp.bfloat16
F32 = jnp.float32
COEF = math.sqrt(2.0 / math.pi)
PLANE = ("y", "x")
SWAP = [(0, 1), (1, 0)]


def gelu_and_slope(z):
    t = jnp.tanh(COEF * (z + 0.044715 * z * z * z))
    value = 0.5 * z * (1.0 + t)
    slope = 0.5 * (1.0 + t) + 0.5 * z * (1.0 - t * t) * COEF * (1.0 + 3.0 * 0.044715 * z * z)
    return value, slope


def dot(a, b):
    return jnp.dot(a, b, preferred_element_type=F32)


def dot_t(a, b):
    return jnp.einsum("tk,nk->tn", a, b, preferred_element_type=F32)


def dot_tok(a, b):
    return jnp.einsum("tm,tn->mn", a, b, preferred_element_type=F32)


def per_device(activations, up_weight, down_weight, cotangent):
    rows, width = activations.shape
    hid = up_weight.shape[1]
    core = lax.axis_index("core")
    zl = lax.axis_index("zl")

    both = jnp.concatenate([activations, cotangent], axis=1)
    panel = lax.all_gather(both, ("zh", "zl"), axis=0, tiled=True)
    tokens = panel.shape[0]
    half = tokens // 2

    def first(part):
        block = lax.dynamic_slice_in_dim(panel, part * half, half, 0)
        pre = dot(block[:, :width], up_weight).astype(BF16)
        grad = dot_t(block[:, width:], down_weight).astype(BF16)
        return jnp.concatenate([pre, grad], axis=1)

    away = first(1 - core)
    arrived = lax.ppermute(away, "core", SWAP)
    home = first(core)
    partial = (home.astype(F32) + arrived.astype(F32)).astype(BF16)

    got = lax.all_to_all(partial, PLANE, 0, 0, tiled=True)
    total = jnp.sum(got.reshape(16, half // 16, 2 * hid).astype(F32), axis=0)
    value, slope = gelu_and_slope(total[:, :hid])
    mine = jnp.concatenate(
        [value.astype(BF16), (total[:, hid:] * slope).astype(BF16)], axis=1
    )
    spread = jnp.broadcast_to(mine[None], (16,) + mine.shape).reshape(half, 2 * hid)
    own_half = lax.all_to_all(spread, PLANE, 0, 0, tiled=True)
    other_half = lax.ppermute(own_half, "core", SWAP)

    def second(block):
        out = dot(block[:, :hid], down_weight).astype(BF16)
        grad = dot_t(block[:, hid:], up_weight).astype(BF16)
        return jnp.concatenate([out, grad], axis=1)

    own_out = second(own_half)
    other_out = second(other_half)
    first_half = jnp.where(core == 0, own_out, other_out)
    second_half = jnp.where(core == 0, other_out, own_out)
    full = jnp.concatenate([first_half, second_half], axis=0)
    pairs = full.reshape(tokens // (2 * rows), 2, rows, 2 * width)
    send = lax.dynamic_index_in_dim(pairs, 1 - zl, 1, keepdims=False)
    keep = lax.dynamic_index_in_dim(pairs, zl, 1, keepdims=False)
    came = lax.ppermute(send, "zl", SWAP)

    hidden_all = jnp.concatenate(
        [jnp.where(core == 0, own_half, other_half), jnp.where(core == 0, other_half, own_half)],
        axis=0,
    )
    grad_down = dot_tok(hidden_all[:, :hid], panel[:, width:]).astype(BF16)
    grad_up = dot_tok(panel[:, :width], hidden_all[:, hid:]).astype(BF16)

    added = (keep.astype(F32) + came.astype(F32)).astype(BF16)
    parts = lax.all_to_all(added.reshape(half, 2 * width), "zh", 0, 0, tiled=True)
    result = jnp.sum(parts.reshape(8, rows, 2 * width).astype(F32), axis=0).astype(BF16)
    return (result[:, :width], result[:, width:], grad_up, grad_down)


def solution(mesh):
    fine = Mesh(mesh.devices.reshape(4, 4, 2, 8, 2), ("y", "x", "core", "zh", "zl"))
    row = ("y", "x", "core")
    col = ("zh", "zl")
    return jax.shard_map(
        per_device,
        mesh=fine,
        in_specs=(P(col, row), P(row, col), P(col, row), P(col, row)),
        out_specs=(P(col, row), P(col, row), P(row, col), P(col, row)),
        check_vma=False,
    )
```

```python
import math

import jax
import jax.numpy as jnp
from jax import lax
from jax.experimental import pallas as pl
from jax.experimental.pallas import tpu as pltpu
from jax.sharding import Mesh
from jax.sharding import PartitionSpec as P

BF16 = jnp.bfloat16
F32 = jnp.float32
COEF = math.sqrt(2.0 / math.pi)
PLANE = ("y", "x")
COL = ("zh", "zl")
SWAP = [(0, 1), (1, 0)]
EVEN = [(z, z ^ 1) for z in range(16)]
ODD = [(z, (((z - 1) ^ 1) + 1) % 16) for z in range(16)]
TILE = 256
PIECES = 4
MIB = 1024 * 1024
VMEM = pl.BlockSpec(memory_space=pltpu.VMEM)
SMEM = pl.BlockSpec(memory_space=pltpu.SMEM)


def gelu_and_slope(z):
    t = jnp.tanh(COEF * (z + 0.044715 * z * z * z))
    value = 0.5 * z * (1.0 + t)
    slope = 0.5 * (1.0 + t) + 0.5 * z * (1.0 - t * t) * COEF * (1.0 + 3.0 * 0.044715 * z * z)
    return value, slope


def matmul(a, b, left, right):
    return lax.dot_general(a, b, (((left,), (right,)), ((), ())), preferred_element_type=F32)


def call(kernel, out_shape, flops, *args, scratch=()):
    specs = [SMEM if a.dtype == jnp.int32 else VMEM for a in args]
    size = sum(a.size * a.dtype.itemsize for a in args) + sum(
        math.prod(o.shape) * o.dtype.itemsize for o in out_shape
    )
    return pl.pallas_call(
        kernel,
        out_shape=out_shape,
        in_specs=specs,
        out_specs=[VMEM] * len(out_shape),
        scratch_shapes=scratch,
        compiler_params=pltpu.CompilerParams(vmem_limit_bytes=10 * MIB),
        cost_estimate=pl.CostEstimate(flops=flops, bytes_accessed=size, transcendentals=0),
    )(*args)


def shape(*dims):
    return jax.ShapeDtypeStruct(dims, BF16)


def pick_kernel(place_ref, pair, out):
    part = out.shape[0]
    rows, cols = 2 * part, pair.shape[1]
    core = place_ref[0]
    mine = pl.multiple_of(core * rows + core * part, part)
    theirs = pl.multiple_of((1 - core) * rows + core * part, part)
    out[:, :cols] = pair[pl.ds(mine, part), :]
    out[:, cols:] = pair[pl.ds(theirs, part), :]


def first_kernel(panel, up, down, up2, down2, out):
    width, hid = up.shape
    act, cot, act2, cot2 = [panel[:, q * width : (q + 1) * width] for q in range(4)]
    for t in range(0, hid, TILE):
        span = slice(t, t + TILE)
        out[:, span] = (
            matmul(act, up[:, span], 1, 0) + matmul(act2, up2[:, span], 1, 0)
        ).astype(BF16)
        out[:, hid + t : hid + t + TILE] = (
            matmul(cot, down[span, :], 1, 1) + matmul(cot2, down2[span, :], 1, 1)
        ).astype(BF16)


def part_rows(place_ref, full, send, keep):
    part = 16
    zl = place_ref[1]
    for q in range(full.shape[0] // (2 * part)):
        base = 2 * q * part
        place = slice(q * part, (q + 1) * part)
        send[place, :] = full[pl.ds(pl.multiple_of(base + (1 - zl) * part, part), part), :]
        keep[place, :] = full[pl.ds(pl.multiple_of(base + zl * part, part), part), :]


def output_kernel(place_ref, block, down, down2, send, keep, full):
    hid, width = down.shape
    full[:, :width] = matmul(block[:, :hid], down[...], 1, 0).astype(BF16)
    full[:, width:] = matmul(block[:, :hid], down2[...], 1, 0).astype(BF16)
    part_rows(place_ref, full, send, keep)


def input_kernel(place_ref, block, up, up2, send, keep, full):
    width, hid = up.shape
    full[:, :width] = matmul(block[:, hid:], up[...], 1, 1).astype(BF16)
    full[:, width:] = matmul(block[:, hid:], up2[...], 1, 1).astype(BF16)
    part_rows(place_ref, full, send, keep)


def pair_kernel(keep_a, came_a, keep_b, came_b, out):
    cols = keep_a.shape[1]
    out[:, :cols] = (keep_a[...].astype(F32) + came_a[...].astype(F32)).astype(BF16)
    out[:, cols:] = (keep_b[...].astype(F32) + came_b[...].astype(F32)).astype(BF16)


def stage_kernel(_, own, panel, *outs):
    *copies, theirs = outs
    cols = copies[0].shape[1]
    for q, copy in enumerate(copies):
        copy[...] = own[:, q * cols : (q + 1) * cols]
    theirs[...] = panel[:, theirs.shape[1] :]


def sum_kernel(parts, out):
    rows = out.shape[0]
    total = parts[:rows, :].astype(F32)
    for q in range(1, parts.shape[0] // rows):
        total = total + parts[q * rows : (q + 1) * rows, :].astype(F32)
    out[...] = total.astype(BF16)


def last_kernel(place_ref, both, output, grad_input):
    rows, width = output.shape
    part = rows // 2
    core = place_ref[0]
    for source in range(2):
        place = slice(source * part, (source + 1) * part)
        own = core == source
        output[place, :] = jnp.where(own, both[place, :width], both[place, width : 2 * width])
        grad_input[place, :] = jnp.where(
            own, both[place, 2 * width : 3 * width], both[place, 3 * width :]
        )


def grads_kernel(panel, panel2, own, *refs):
    *others, grad_up, grad_down = refs
    width, hid = grad_up.shape
    act, cot = panel[:, :width], panel[:, width : 2 * width]
    act2, cot2 = panel2[:, :width], panel2[:, width:]
    piece = others[0].shape[1]

    def other(begin):
        return others[begin // piece][:, begin % piece : begin % piece + TILE]

    for j in range(0, hid, TILE):
        grad_down[j : j + TILE, :] = (
            matmul(own[:, j : j + TILE], cot, 0, 0) + matmul(other(j), cot2, 0, 0)
        ).astype(BF16)
        grad_up[:, j : j + TILE] = (
            matmul(act, own[:, hid + j : hid + j + TILE], 0, 0)
            + matmul(act2, other(hid + j), 0, 0)
        ).astype(BF16)


def per_device(activations, up, down, cotangent):
    rows, width = activations.shape
    hid = up.shape[1]
    place = jnp.stack([lax.axis_index("core"), lax.axis_index("zl")]).astype(jnp.int32)
    part = rows // 2
    half = 16 * part
    members = 16
    work = 8 * half * width * hid

    up2 = lax.ppermute(up, "core", SWAP)
    down2 = lax.ppermute(down, "core", SWAP)
    pair = lax.all_gather(
        jnp.concatenate([activations, cotangent], axis=1), "core", axis=0, tiled=True
    )
    (mine,) = call(pick_kernel, [shape(part, 4 * width)], 0, place, pair)
    panel = lax.all_gather(mine, COL, axis=0, tiled=True)

    (partial,) = call(
        first_kernel, [shape(half, 2 * hid)], work, panel, up, down, up2, down2
    )

    got = lax.all_to_all(partial, PLANE, 0, 0, tiled=True)
    total = jnp.sum(got.reshape(members, half // members, 2 * hid).astype(F32), axis=0)
    value, slope = gelu_and_slope(total[:, :hid])
    sixteen = jnp.concatenate(
        [value.astype(BF16), (total[:, hid:] * slope).astype(BF16)], axis=1
    )
    spread = jnp.broadcast_to(sixteen[None], (members,) + sixteen.shape).reshape(half, 2 * hid)
    own = lax.all_to_all(spread, PLANE, 0, 0, tiled=True)

    def second(kernel, *args):
        outs = [shape(half // 2, 2 * width)] * 2
        return call(kernel, outs, work // 2, *args, scratch=[pltpu.VMEM((half, 2 * width), BF16)])

    send_out, keep_out = second(output_kernel, place, own, down, down2)
    came_out = lax.ppermute(send_out, COL, EVEN)
    send_in, keep_in = second(input_kernel, place, own, up, up2)
    came_in = lax.ppermute(send_in, COL, ODD)
    (added,) = call(
        pair_kernel, [shape(half // 2, 4 * width)], 0, keep_out, came_out, keep_in, came_in
    )
    gathered = lax.all_to_all(added, "zh", 0, 0, tiled=True)

    pieces = call(
        stage_kernel, [shape(half, 2 * width)] * (PIECES + 1), work // 4, added, own, panel
    )
    *others, panel2 = [lax.ppermute(piece, "core", SWAP) for piece in pieces]
    grad_up, grad_down = call(
        grads_kernel,
        [shape(width, hid), shape(hid, width)],
        work,
        panel,
        panel2,
        own,
        *others,
    )

    gathered, grad_up, grad_down = lax.optimization_barrier((gathered, grad_up, grad_down))
    (summed,) = call(sum_kernel, [shape(part, 4 * width)], 0, gathered)
    both = lax.all_gather(summed, "core", axis=0, tiled=True)
    output, grad_input = call(last_kernel, [shape(rows, width)] * 2, 0, place, both)
    return (output, grad_input, grad_up, grad_down)


def solution(mesh):
    fine = Mesh(mesh.devices.reshape(4, 4, 2, 8, 2), ("y", "x", "core", "zh", "zl"))
    row = ("y", "x", "core")
    return jax.shard_map(
        per_device,
        mesh=fine,
        in_specs=(P(COL, row), P(row, COL), P(COL, row), P(COL, row)),
        out_specs=(P(COL, row), P(COL, row), P(row, COL), P(COL, row)),
        check_vma=False,
    )
```

```python
import functools
import math

import jax
import jax.numpy as jnp
from jax import lax
from jax.experimental import pallas as pl
from jax.experimental.pallas import tpu as pltpu
from jax.sharding import Mesh
from jax.sharding import PartitionSpec as P

BF16 = jnp.bfloat16
F32 = jnp.float32
COEF = math.sqrt(2.0 / math.pi)
PLANE = ("y", "x")
COL = ("zh", "zl")
SWAP = [(0, 1), (1, 0)]
EVEN = [(z, z ^ 1) for z in range(16)]
ODD = [(z, (((z - 1) ^ 1) + 1) % 16) for z in range(16)]
TILE = 256
PIECES = 3
MIB = 1024 * 1024
VMEM = pl.BlockSpec(memory_space=pltpu.VMEM)
SMEM = pl.BlockSpec(memory_space=pltpu.SMEM)


def gelu_and_slope(z):
    t = jnp.tanh(COEF * (z + 0.044715 * z * z * z))
    value = 0.5 * z * (1.0 + t)
    slope = 0.5 * (1.0 + t) + 0.5 * z * (1.0 - t * t) * COEF * (1.0 + 3.0 * 0.044715 * z * z)
    return value, slope


def matmul(a, b, left, right):
    return lax.dot_general(a, b, (((left,), (right,)), ((), ())), preferred_element_type=F32)


def call(kernel, out_shape, flops, *args, scratch=()):
    specs = [SMEM if a.dtype == jnp.int32 else VMEM for a in args]
    size = sum(a.size * a.dtype.itemsize for a in args) + sum(
        math.prod(o.shape) * o.dtype.itemsize for o in out_shape
    )
    return pl.pallas_call(
        kernel,
        out_shape=out_shape,
        in_specs=specs,
        out_specs=[VMEM] * len(out_shape),
        scratch_shapes=scratch,
        compiler_params=pltpu.CompilerParams(vmem_limit_bytes=10 * MIB),
        cost_estimate=pl.CostEstimate(flops=flops, bytes_accessed=size, transcendentals=0),
    )(*args)


def shape(*dims):
    return jax.ShapeDtypeStruct(dims, BF16)


def pick_kernel(core_ref, _, pair, out):
    part = out.shape[0]
    rows, cols = 2 * part, pair.shape[1]
    core = core_ref[0]
    mine = pl.multiple_of(core * rows + core * part, part)
    theirs = pl.multiple_of((1 - core) * rows + core * part, part)
    out[:, :cols] = pair[pl.ds(mine, part), :]
    out[:, cols:] = pair[pl.ds(theirs, part), :]


def first_kernel(panel, up, down, up2, down2, out):
    width, hid = up.shape
    act, cot, act2, cot2 = [panel[:, q * width : (q + 1) * width] for q in range(4)]
    for t in range(0, hid, TILE):
        span = slice(t, t + TILE)
        out[:, span] = (
            matmul(act, up[:, span], 1, 0) + matmul(act2, up2[:, span], 1, 0)
        ).astype(BF16)
        out[:, hid + t : hid + t + TILE] = (
            matmul(cot, down[span, :], 1, 1) + matmul(cot2, down2[span, :], 1, 1)
        ).astype(BF16)


def middle_kernel(got, spread):
    members = 16
    part = got.shape[0] // members
    hid = got.shape[1] // 2

    def summed(cols):
        total = got[:part, cols].astype(F32)
        for q in range(1, members):
            total = total + got[q * part : (q + 1) * part, cols].astype(F32)
        return total

    for t in range(0, hid, TILE):
        here, there = slice(t, t + TILE), slice(hid + t, hid + t + TILE)
        value, slope = gelu_and_slope(summed(here))
        value = value.astype(BF16)
        slope = (summed(there) * slope).astype(BF16)
        for q in range(members):
            spread[q * part : (q + 1) * part, here] = value
            spread[q * part : (q + 1) * part, there] = slope


def second_kernel(flip, zl_ref, block, up, down, up2, down2, output, grad_input, rows):
    width, hid = up.shape
    part = 16
    parity = 1 - zl_ref[0] if flip else zl_ref[0]
    for q in range(rows.shape[0] // part):
        begin = pl.multiple_of((2 * q + parity) * part, part)
        rows[q * part : (q + 1) * part, :] = block[pl.ds(begin, part), :]
    output[:, :width] = matmul(rows[:, :hid], down[...], 1, 0).astype(BF16)
    output[:, width:] = matmul(rows[:, :hid], down2[...], 1, 0).astype(BF16)
    grad_input[:, :width] = matmul(rows[:, hid:], up[...], 1, 1).astype(BF16)
    grad_input[:, width:] = matmul(rows[:, hid:], up2[...], 1, 1).astype(BF16)


def pair_kernel(keep_a, came_a, keep_b, came_b, out):
    cols = keep_a.shape[1]
    out[:, :cols] = (keep_a[...].astype(F32) + came_a[...].astype(F32)).astype(BF16)
    out[:, cols:] = (keep_b[...].astype(F32) + came_b[...].astype(F32)).astype(BF16)


def stage_kernel(_, own, panel, *outs):
    cols = outs[0].shape[1]
    split = own.shape[1]
    for q, out in enumerate(outs):
        begin, end = q * cols, (q + 1) * cols
        if end <= split:
            out[...] = own[:, begin:end]
        else:
            rest = panel.shape[1] // 2 + begin - split
            if begin < split:
                out[:, : split - begin] = own[:, begin:]
                rest = panel.shape[1] // 2
            out[:, max(split - begin, 0) :] = panel[:, rest : rest + end - max(split, begin)]


def sum_kernel(parts, out):
    rows = out.shape[0]
    total = parts[:rows, :].astype(F32)
    for q in range(1, parts.shape[0] // rows):
        total = total + parts[q * rows : (q + 1) * rows, :].astype(F32)
    out[...] = total.astype(BF16)


def last_kernel(core_ref, both, output, grad_input):
    rows, width = output.shape
    part = rows // 2
    core = core_ref[0]
    for source in range(2):
        place = slice(source * part, (source + 1) * part)
        own = core == source
        output[place, :] = jnp.where(own, both[place, :width], both[place, width : 2 * width])
        grad_input[place, :] = jnp.where(
            own, both[place, 2 * width : 3 * width], both[place, 3 * width :]
        )


def grads_kernel(panel, own, *refs):
    *others, grad_up, grad_down = refs
    width, hid = grad_up.shape
    piece = others[0].shape[1]

    def other(begin, size):
        return others[begin // piece][:, begin % piece : begin % piece + size]

    act, cot = panel[:, :width], panel[:, width : 2 * width]
    act2, cot2 = other(2 * hid, width), other(2 * hid + width, width)
    for j in range(0, hid, TILE):
        grad_down[j : j + TILE, :] = (
            matmul(own[:, j : j + TILE], cot, 0, 0) + matmul(other(j, TILE), cot2, 0, 0)
        ).astype(BF16)
        grad_up[:, j : j + TILE] = (
            matmul(act, own[:, hid + j : hid + j + TILE], 0, 0)
            + matmul(act2, other(hid + j, TILE), 0, 0)
        ).astype(BF16)


def per_device(activations, up, down, cotangent):
    rows, width = activations.shape
    hid = up.shape[1]
    core = lax.axis_index("core").astype(jnp.int32).reshape(1)
    zl = lax.axis_index("zl").astype(jnp.int32).reshape(1)
    part = rows // 2
    half = 16 * part
    members = 16
    work = 8 * half * width * hid

    up2 = lax.ppermute(up, "core", SWAP)
    down2 = lax.ppermute(down, "core", SWAP)
    pair = lax.all_gather(
        jnp.concatenate([activations, cotangent], axis=1), "core", axis=0, tiled=True
    )
    (mine,) = call(pick_kernel, [shape(part, 4 * width)], 8 * work, core, zl, pair)
    panel = lax.all_gather(mine, COL, axis=0, tiled=True)

    (partial,) = call(
        first_kernel, [shape(half, 2 * hid)], work, panel, up, down, up2, down2
    )

    got = lax.all_to_all(partial, PLANE, 0, 0, tiled=True)
    (spread,) = call(middle_kernel, [shape(half, 2 * hid)], 8 * work, got)
    own = lax.all_to_all(spread, PLANE, 0, 0, tiled=True)

    def second(flip):
        return call(
            functools.partial(second_kernel, flip),
            [shape(half // 2, 2 * width)] * 2,
            work // 2,
            zl,
            own,
            up,
            down,
            up2,
            down2,
            scratch=[pltpu.VMEM((half // 2, 2 * hid), BF16)],
        )

    send_out, send_in = second(True)
    came_out = lax.ppermute(send_out, COL, EVEN)
    came_in = lax.ppermute(send_in, COL, ODD)
    keep_out, keep_in = second(False)
    (added,) = call(
        pair_kernel, [shape(half // 2, 4 * width)], 0, keep_out, came_out, keep_in, came_in
    )
    gathered = lax.all_to_all(added, "zh", 0, 0, tiled=True)

    piece = (2 * hid + 2 * width) // PIECES
    pieces = call(stage_kernel, [shape(half, piece)] * PIECES, work // 4, added, own, panel)
    others = [lax.ppermute(piece, "core", SWAP) for piece in pieces]
    grad_up, grad_down = call(
        grads_kernel, [shape(width, hid), shape(hid, width)], work, panel, own, *others
    )

    gathered, grad_up, grad_down = lax.optimization_barrier((gathered, grad_up, grad_down))
    (summed,) = call(sum_kernel, [shape(part, 4 * width)], 0, gathered)
    both = lax.all_gather(summed, "core", axis=0, tiled=True)
    output, grad_input = call(last_kernel, [shape(rows, width)] * 2, 0, core, both)
    return (output, grad_input, grad_up, grad_down)


def solution(mesh):
    fine = Mesh(mesh.devices.reshape(4, 4, 2, 8, 2), ("y", "x", "core", "zh", "zl"))
    row = ("y", "x", "core")
    return jax.shard_map(
        per_device,
        mesh=fine,
        in_specs=(P(COL, row), P(row, COL), P(COL, row), P(COL, row)),
        out_specs=(P(COL, row), P(COL, row), P(row, COL), P(COL, row)),
        check_vma=False,
    )
```

```python
import functools
import math

import jax
import jax.numpy as jnp
from jax import lax
from jax.experimental import pallas as pl
from jax.experimental.pallas import tpu as pltpu
from jax.sharding import Mesh
from jax.sharding import PartitionSpec as P

BF16 = jnp.bfloat16
F32 = jnp.float32
COEF = math.sqrt(2.0 / math.pi)
PLANE = ("y", "x")
TURN = 12
RING = [(z + TURN) % 16 for z in range(16)]
SHIFT = 4
PARITIES = [[(TURN + p * (2 * SHIFT + 1) + 2 * q) % 16 for q in range(8)] for p in range(2)]
SWAP = [(0, 1), (1, 0)]
EVEN = [(z, z ^ 1) for z in range(16)]
ODD = [(z, (((z - 1) ^ 1) + 1) % 16) for z in range(16)]
TILE = 256
PIECES = 3
MIB = 1024 * 1024
VMEM = pl.BlockSpec(memory_space=pltpu.VMEM)
SMEM = pl.BlockSpec(memory_space=pltpu.SMEM)


def gelu_and_slope(z):
    t = jnp.tanh(COEF * (z + 0.044715 * z * z * z))
    value = 0.5 * z * (1.0 + t)
    slope = 0.5 * (1.0 + t) + 0.5 * z * (1.0 - t * t) * COEF * (1.0 + 3.0 * 0.044715 * z * z)
    return value, slope


def matmul(a, b, left, right):
    return lax.dot_general(a, b, (((left,), (right,)), ((), ())), preferred_element_type=F32)


def call(kernel, out_shape, flops, *args, scratch=()):
    specs = [SMEM if a.dtype == jnp.int32 else VMEM for a in args]
    size = sum(a.size * a.dtype.itemsize for a in args) + sum(
        math.prod(o.shape) * o.dtype.itemsize for o in out_shape
    )
    return pl.pallas_call(
        kernel,
        out_shape=out_shape,
        in_specs=specs,
        out_specs=[VMEM] * len(out_shape),
        scratch_shapes=scratch,
        compiler_params=pltpu.CompilerParams(vmem_limit_bytes=10 * MIB),
        cost_estimate=pl.CostEstimate(flops=flops, bytes_accessed=size, transcendentals=0),
    )(*args)


def shape(*dims):
    return jax.ShapeDtypeStruct(dims, BF16)


def pick_kernel(core_ref, _, pair, out):
    part = out.shape[0]
    rows, cols = 2 * part, pair.shape[1]
    core = core_ref[0]
    mine = pl.multiple_of(core * rows + core * part, part)
    theirs = pl.multiple_of((1 - core) * rows + core * part, part)
    out[:, :cols] = pair[pl.ds(mine, part), :]
    out[:, cols:] = pair[pl.ds(theirs, part), :]


def first_kernel(panel, up, down, up2, down2, out):
    width, hid = up.shape
    act, cot, act2, cot2 = [panel[:, q * width : (q + 1) * width] for q in range(4)]
    for t in range(0, hid, TILE):
        span = slice(t, t + TILE)
        out[:, span] = (
            matmul(act, up[:, span], 1, 0) + matmul(act2, up2[:, span], 1, 0)
        ).astype(BF16)
        out[:, hid + t : hid + t + TILE] = (
            matmul(cot, down[span, :], 1, 1) + matmul(cot2, down2[span, :], 1, 1)
        ).astype(BF16)


def middle_kernel(got, spread):
    members = 16
    part = got.shape[0] // members
    hid = got.shape[1] // 2

    def summed(cols):
        total = got[:part, cols].astype(F32)
        for q in range(1, members):
            total = total + got[q * part : (q + 1) * part, cols].astype(F32)
        return total

    for t in range(0, hid, TILE):
        here, there = slice(t, t + TILE), slice(hid + t, hid + t + TILE)
        value, slope = gelu_and_slope(summed(here))
        value = value.astype(BF16)
        slope = (summed(there) * slope).astype(BF16)
        for q in range(members):
            spread[q * part : (q + 1) * part, here] = value
            spread[q * part : (q + 1) * part, there] = slope


def second_kernel(flip, zl_ref, block, up, down, up2, down2, output, grad_input, rows):
    width, hid = up.shape
    part = 16
    parity = 1 - zl_ref[0] if flip else zl_ref[0]
    for q in range(rows.shape[0] // part):
        block_at = 2 * lax.rem(q + SHIFT * parity, 8) + parity
        begin = pl.multiple_of(block_at * part, part)
        rows[q * part : (q + 1) * part, :] = block[pl.ds(begin, part), :]
    output[:, :width] = matmul(rows[:, :hid], down[...], 1, 0).astype(BF16)
    output[:, width:] = matmul(rows[:, :hid], down2[...], 1, 0).astype(BF16)
    grad_input[:, :width] = matmul(rows[:, hid:], up[...], 1, 1).astype(BF16)
    grad_input[:, width:] = matmul(rows[:, hid:], up2[...], 1, 1).astype(BF16)


def pair_kernel(keep_a, came_a, keep_b, came_b, out):
    cols = keep_a.shape[1]
    out[:, :cols] = (keep_a[...].astype(F32) + came_a[...].astype(F32)).astype(BF16)
    out[:, cols:] = (keep_b[...].astype(F32) + came_b[...].astype(F32)).astype(BF16)


def stage_kernel(_, own, panel, *outs):
    cols = outs[0].shape[1]
    split = own.shape[1]
    for q, out in enumerate(outs):
        begin, end = q * cols, (q + 1) * cols
        if end <= split:
            out[...] = own[:, begin:end]
        else:
            rest = panel.shape[1] // 2 + begin - split
            if begin < split:
                out[:, : split - begin] = own[:, begin:]
                rest = panel.shape[1] // 2
            out[:, max(split - begin, 0) :] = panel[:, rest : rest + end - max(split, begin)]


def sum_kernel(parts, out):
    rows = out.shape[0]
    total = parts[:rows, :].astype(F32)
    for q in range(1, parts.shape[0] // rows):
        total = total + parts[q * rows : (q + 1) * rows, :].astype(F32)
    out[...] = total.astype(BF16)


def last_kernel(core_ref, both, output, grad_input):
    rows, width = output.shape
    part = rows // 2
    core = core_ref[0]
    for source in range(2):
        place = slice(source * part, (source + 1) * part)
        own = core == source
        output[place, :] = jnp.where(own, both[place, :width], both[place, width : 2 * width])
        grad_input[place, :] = jnp.where(
            own, both[place, 2 * width : 3 * width], both[place, 3 * width :]
        )


def grads_kernel(panel, own, *refs):
    *others, grad_up, grad_down = refs
    width, hid = grad_up.shape
    piece = others[0].shape[1]

    def other(begin, size):
        return others[begin // piece][:, begin % piece : begin % piece + size]

    act, cot = panel[:, :width], panel[:, width : 2 * width]
    act2, cot2 = other(2 * hid, width), other(2 * hid + width, width)
    for j in range(0, hid, TILE):
        grad_down[j : j + TILE, :] = (
            matmul(own[:, j : j + TILE], cot, 0, 0) + matmul(other(j, TILE), cot2, 0, 0)
        ).astype(BF16)
        grad_up[:, j : j + TILE] = (
            matmul(act, own[:, hid + j : hid + j + TILE], 0, 0)
            + matmul(act2, other(hid + j, TILE), 0, 0)
        ).astype(BF16)


def per_device(activations, up, down, cotangent):
    rows, width = activations.shape
    hid = up.shape[1]
    core = lax.axis_index("core").astype(jnp.int32).reshape(1)
    zl = (lax.axis_index("col") % 2).astype(jnp.int32).reshape(1)
    part = rows // 2
    half = 16 * part
    members = 16
    work = 8 * half * width * hid

    up2 = lax.ppermute(up, "core", SWAP)
    down2 = lax.ppermute(down, "core", SWAP)
    pair = lax.all_gather(
        jnp.concatenate([activations, cotangent], axis=1), "core", axis=0, tiled=True
    )
    (mine,) = call(pick_kernel, [shape(part, 4 * width)], 8 * work, core, zl, pair)
    panel = lax.all_gather(mine, "col", axis=0, tiled=True, axis_index_groups=[RING])

    (partial,) = call(
        first_kernel, [shape(half, 2 * hid)], work, panel, up, down, up2, down2
    )

    got = lax.all_to_all(partial, PLANE, 0, 0, tiled=True)
    (spread,) = call(middle_kernel, [shape(half, 2 * hid)], 8 * work, got)
    own = lax.all_to_all(spread, PLANE, 0, 0, tiled=True)

    def second(flip):
        return call(
            functools.partial(second_kernel, flip),
            [shape(half // 2, 2 * width)] * 2,
            work // 2,
            zl,
            own,
            up,
            down,
            up2,
            down2,
            scratch=[pltpu.VMEM((half // 2, 2 * hid), BF16)],
        )

    send_out, send_in = second(True)
    came_out = lax.ppermute(send_out, "col", EVEN)
    came_in = lax.ppermute(send_in, "col", ODD)
    keep_out, keep_in = second(False)
    (added,) = call(
        pair_kernel, [shape(half // 2, 4 * width)], 0, keep_out, came_out, keep_in, came_in
    )
    gathered = lax.all_to_all(
        added, "col", 0, 0, tiled=True, axis_index_groups=PARITIES
    )

    piece = (2 * hid + 2 * width) // PIECES
    pieces = call(stage_kernel, [shape(half, piece)] * PIECES, work // 4, added, own, panel)
    others = [lax.ppermute(piece, "core", SWAP) for piece in pieces]
    grad_up, grad_down = call(
        grads_kernel, [shape(width, hid), shape(hid, width)], work, panel, own, *others
    )

    gathered, grad_up, grad_down = lax.optimization_barrier((gathered, grad_up, grad_down))
    (summed,) = call(sum_kernel, [shape(part, 4 * width)], 0, gathered)
    both = lax.all_gather(summed, "core", axis=0, tiled=True)
    output, grad_input = call(last_kernel, [shape(rows, width)] * 2, 0, core, both)
    return (output, grad_input, grad_up, grad_down)


def solution(mesh):
    fine = Mesh(mesh.devices.reshape(4, 4, 2, 16), ("y", "x", "core", "col"))
    row = ("y", "x", "core")
    return jax.shard_map(
        per_device,
        mesh=fine,
        in_specs=(P("col", row), P(row, "col"), P("col", row), P("col", row)),
        out_specs=(P("col", row), P("col", row), P(row, "col"), P("col", row)),
        check_vma=False,
    )
```

```python
import functools
import math

import jax
import jax.numpy as jnp
from jax import lax
from jax.experimental import pallas as pl
from jax.experimental.pallas import tpu as pltpu
from jax.sharding import Mesh
from jax.sharding import PartitionSpec as P

BF16 = jnp.bfloat16
F32 = jnp.float32
COEF = math.sqrt(2.0 / math.pi)
CHIPS = [list(range(15, -1, -1))]
TURN = 12
RING = [(z + TURN) % 16 for z in range(16)]
SHIFT = 4
PARITIES = [[(TURN + p * (2 * SHIFT + 1) + 2 * q) % 16 for q in range(8)] for p in range(2)]
SWAP = [(0, 1), (1, 0)]
EVEN = [(z, z ^ 1) for z in range(16)]
ODD = [(z, (((z - 1) ^ 1) + 1) % 16) for z in range(16)]
TILE = 256
MIB = 1024 * 1024
VMEM = pl.BlockSpec(memory_space=pltpu.VMEM)
SMEM = pl.BlockSpec(memory_space=pltpu.SMEM)


def gelu_and_slope(z):
    t = jnp.tanh(COEF * (z + 0.044715 * z * z * z))
    value = 0.5 * z * (1.0 + t)
    slope = 0.5 * (1.0 + t) + 0.5 * z * (1.0 - t * t) * COEF * (1.0 + 3.0 * 0.044715 * z * z)
    return value, slope


def matmul(a, b, left, right):
    return lax.dot_general(a, b, (((left,), (right,)), ((), ())), preferred_element_type=F32)


def call(kernel, out_shape, flops, *args, scratch=()):
    specs = [SMEM if a.dtype == jnp.int32 else VMEM for a in args]
    size = sum(a.size * a.dtype.itemsize for a in args) + sum(
        math.prod(o.shape) * o.dtype.itemsize for o in out_shape
    )
    return pl.pallas_call(
        kernel,
        out_shape=out_shape,
        in_specs=specs,
        out_specs=[VMEM] * len(out_shape),
        scratch_shapes=scratch,
        compiler_params=pltpu.CompilerParams(vmem_limit_bytes=10 * MIB),
        cost_estimate=pl.CostEstimate(flops=flops, bytes_accessed=size, transcendentals=0),
    )(*args)


def shape(*dims):
    return jax.ShapeDtypeStruct(dims, BF16)


def pick_kernel(core_ref, _, pair, out):
    part = out.shape[0]
    rows, cols = 2 * part, pair.shape[1]
    core = core_ref[0]
    mine = pl.multiple_of(core * rows + core * part, part)
    theirs = pl.multiple_of((1 - core) * rows + core * part, part)
    out[:, :cols] = pair[pl.ds(mine, part), :]
    out[:, cols:] = pair[pl.ds(theirs, part), :]


def first_kernel(panel, up, down, up2, down2, out):
    width, hid = up.shape
    act, cot, act2, cot2 = [panel[:, q * width : (q + 1) * width] for q in range(4)]
    for t in range(0, hid, TILE):
        span = slice(t, t + TILE)
        out[:, span] = (
            matmul(act, up[:, span], 1, 0) + matmul(act2, up2[:, span], 1, 0)
        ).astype(BF16)
        out[:, hid + t : hid + t + TILE] = (
            matmul(cot, down[span, :], 1, 1) + matmul(cot2, down2[span, :], 1, 1)
        ).astype(BF16)


def middle_kernel(got, spread):
    members = 16
    part = got.shape[0] // members
    hid = got.shape[1] // 2

    def summed(cols):
        total = got[:part, cols].astype(F32)
        for q in range(1, members):
            total = total + got[q * part : (q + 1) * part, cols].astype(F32)
        return total

    for t in range(0, hid, TILE):
        here, there = slice(t, t + TILE), slice(hid + t, hid + t + TILE)
        value, slope = gelu_and_slope(summed(here))
        value = value.astype(BF16)
        slope = (summed(there) * slope).astype(BF16)
        for q in range(members):
            spread[q * part : (q + 1) * part, here] = value
            spread[q * part : (q + 1) * part, there] = slope


def second_kernel(flip, zl_ref, block, up, down, up2, down2, output, grad_input, rows):
    width, hid = up.shape
    part = 16
    parity = 1 - zl_ref[0] if flip else zl_ref[0]
    for q in range(rows.shape[0] // part):
        block_at = 2 * lax.rem(q + SHIFT * parity, 8) + parity
        begin = pl.multiple_of(block_at * part, part)
        rows[q * part : (q + 1) * part, :] = block[pl.ds(begin, part), :]
    output[:, :width] = matmul(rows[:, :hid], down[...], 1, 0).astype(BF16)
    output[:, width:] = matmul(rows[:, :hid], down2[...], 1, 0).astype(BF16)
    grad_input[:, :width] = matmul(rows[:, hid:], up[...], 1, 1).astype(BF16)
    grad_input[:, width:] = matmul(rows[:, hid:], up2[...], 1, 1).astype(BF16)


def pair_kernel(keep_a, came_a, keep_b, came_b, out):
    cols = keep_a.shape[1]
    out[:, :cols] = (keep_a[...].astype(F32) + came_a[...].astype(F32)).astype(BF16)
    out[:, cols:] = (keep_b[...].astype(F32) + came_b[...].astype(F32)).astype(BF16)


def stage_kernel(_, own, panel, first, second):
    hid = own.shape[1] // 2
    width = panel.shape[1] // 4
    first[:, :hid] = own[:, :hid]
    first[:, hid:] = panel[:, 3 * width :]
    second[:, :hid] = own[:, hid:]
    second[:, hid:] = panel[:, 2 * width : 3 * width]


def sum_kernel(parts, out):
    rows = out.shape[0]
    total = parts[:rows, :].astype(F32)
    for q in range(1, parts.shape[0] // rows):
        total = total + parts[q * rows : (q + 1) * rows, :].astype(F32)
    out[...] = total.astype(BF16)


def last_kernel(core_ref, both, output, grad_input):
    rows, width = output.shape
    part = rows // 2
    core = core_ref[0]
    for source in range(2):
        place = slice(source * part, (source + 1) * part)
        own = core == source
        output[place, :] = jnp.where(own, both[place, :width], both[place, width : 2 * width])
        grad_input[place, :] = jnp.where(
            own, both[place, 2 * width : 3 * width], both[place, 3 * width :]
        )


def grads_kernel(panel, own, first, second, grad_up, grad_down):
    width, hid = grad_up.shape
    act, cot = panel[:, :width], panel[:, width : 2 * width]
    act2, cot2 = second[:, hid:], first[:, hid:]
    for j in range(0, hid, TILE):
        cols = slice(j, j + TILE)
        grad_down[cols, :] = (
            matmul(own[:, cols], cot, 0, 0) + matmul(first[:, cols], cot2, 0, 0)
        ).astype(BF16)
        grad_up[:, cols] = (
            matmul(act, own[:, hid + j : hid + j + TILE], 0, 0)
            + matmul(act2, second[:, cols], 0, 0)
        ).astype(BF16)


def per_device(activations, up, down, cotangent):
    rows, width = activations.shape
    hid = up.shape[1]
    core = lax.axis_index("core").astype(jnp.int32).reshape(1)
    zl = (lax.axis_index("col") % 2).astype(jnp.int32).reshape(1)
    part = rows // 2
    half = 16 * part
    members = 16
    work = 8 * half * width * hid

    up2 = lax.ppermute(up, "core", SWAP)
    down2 = lax.ppermute(down, "core", SWAP)
    pair = lax.all_gather(
        jnp.concatenate([activations, cotangent], axis=1), "core", axis=0, tiled=True
    )
    (mine,) = call(pick_kernel, [shape(part, 4 * width)], 8 * work, core, zl, pair)
    panel = lax.all_gather(mine, "col", axis=0, tiled=True, axis_index_groups=[RING])

    (partial,) = call(
        first_kernel, [shape(half, 2 * hid)], work, panel, up, down, up2, down2
    )

    got = lax.all_to_all(partial, "plane", 0, 0, tiled=True, axis_index_groups=CHIPS)
    (spread,) = call(middle_kernel, [shape(half, 2 * hid)], 8 * work, got)
    own = lax.all_to_all(spread, "plane", 0, 0, tiled=True, axis_index_groups=CHIPS)

    def second(flip):
        return call(
            functools.partial(second_kernel, flip),
            [shape(half // 2, 2 * width)] * 2,
            work // 2,
            zl,
            own,
            up,
            down,
            up2,
            down2,
            scratch=[pltpu.VMEM((half // 2, 2 * hid), BF16)],
        )

    send_out, send_in = second(True)
    came_out = lax.ppermute(send_out, "col", EVEN)
    came_in = lax.ppermute(send_in, "col", ODD)
    keep_out, keep_in = second(False)
    (added,) = call(
        pair_kernel, [shape(half // 2, 4 * width)], 0, keep_out, came_out, keep_in, came_in
    )
    gathered = lax.all_to_all(
        added, "col", 0, 0, tiled=True, axis_index_groups=PARITIES
    )

    pieces = call(
        stage_kernel, [shape(half, hid + width)] * 2, work // 4, added, own, panel
    )
    others = [lax.ppermute(piece, "core", SWAP) for piece in pieces]
    grad_up, grad_down = call(
        grads_kernel, [shape(width, hid), shape(hid, width)], work, panel, own, *others
    )

    gathered, grad_up, grad_down = lax.optimization_barrier((gathered, grad_up, grad_down))
    (summed,) = call(sum_kernel, [shape(part, 4 * width)], 0, gathered)
    both = lax.all_gather(summed, "core", axis=0, tiled=True)
    output, grad_input = call(last_kernel, [shape(rows, width)] * 2, 0, core, both)
    return (output, grad_input, grad_up, grad_down)


def solution(mesh):
    fine = Mesh(mesh.devices.reshape(16, 2, 16), ("plane", "core", "col"))
    row = ("plane", "core")
    return jax.shard_map(
        per_device,
        mesh=fine,
        in_specs=(P("col", row), P(row, "col"), P("col", row), P("col", row)),
        out_specs=(P("col", row), P("col", row), P(row, "col"), P("col", row)),
        check_vma=False,
    )
```

```python
import functools
import math

import jax
import jax.numpy as jnp
from jax import lax
from jax.experimental import pallas as pl
from jax.experimental.pallas import tpu as pltpu
from jax.sharding import Mesh
from jax.sharding import PartitionSpec as P

BF16 = jnp.bfloat16
F32 = jnp.float32
COEF = math.sqrt(2.0 / math.pi)
CHIPS = [list(range(15, -1, -1))]
TURN = 12
RING = [(z + TURN) % 16 for z in range(16)]
SHIFT = 4
PARITIES = [[(TURN + p * (2 * SHIFT + 1) + 2 * q) % 16 for q in range(8)] for p in range(2)]
SWAP = [(0, 1), (1, 0)]
EVEN = [(z, z ^ 1) for z in range(16)]
TILE = 256
MIB = 1024 * 1024
VMEM = pl.BlockSpec(memory_space=pltpu.VMEM)
SMEM = pl.BlockSpec(memory_space=pltpu.SMEM)


def gelu_and_slope(z):
    t = jnp.tanh(COEF * (z + 0.044715 * z * z * z))
    value = 0.5 * z * (1.0 + t)
    slope = 0.5 * (1.0 + t) + 0.5 * z * (1.0 - t * t) * COEF * (1.0 + 3.0 * 0.044715 * z * z)
    return value, slope


def matmul(a, b, left, right):
    return lax.dot_general(a, b, (((left,), (right,)), ((), ())), preferred_element_type=F32)


def call(kernel, out_shape, flops, *args, scratch=()):
    specs = [SMEM if a.dtype == jnp.int32 else VMEM for a in args]
    size = sum(a.size * a.dtype.itemsize for a in args) + sum(
        math.prod(o.shape) * o.dtype.itemsize for o in out_shape
    )
    return pl.pallas_call(
        kernel,
        out_shape=out_shape,
        in_specs=specs,
        out_specs=[VMEM] * len(out_shape),
        scratch_shapes=scratch,
        compiler_params=pltpu.CompilerParams(vmem_limit_bytes=10 * MIB),
        cost_estimate=pl.CostEstimate(flops=flops, bytes_accessed=size, transcendentals=0),
    )(*args)


def shape(*dims):
    return jax.ShapeDtypeStruct(dims, BF16)


def pick_kernel(core_ref, _, pair, out):
    part = out.shape[0]
    rows, cols = 2 * part, pair.shape[1]
    core = core_ref[0]
    mine = pl.multiple_of(core * rows + core * part, part)
    theirs = pl.multiple_of((1 - core) * rows + core * part, part)
    out[:, :cols] = pair[pl.ds(mine, part), :]
    out[:, cols:] = pair[pl.ds(theirs, part), :]


def first_kernel(panel, up, down, up2, down2, out):
    width, hid = up.shape
    act, cot, act2, cot2 = [panel[:, q * width : (q + 1) * width] for q in range(4)]
    for t in range(0, hid, TILE):
        span = slice(t, t + TILE)
        out[:, span] = (
            matmul(act, up[:, span], 1, 0) + matmul(act2, up2[:, span], 1, 0)
        ).astype(BF16)
        out[:, hid + t : hid + t + TILE] = (
            matmul(cot, down[span, :], 1, 1) + matmul(cot2, down2[span, :], 1, 1)
        ).astype(BF16)


def middle_kernel(got, spread):
    members = 16
    part = got.shape[0] // members
    hid = got.shape[1] // 2

    def summed(cols):
        total = got[:part, cols].astype(F32)
        for q in range(1, members):
            total = total + got[q * part : (q + 1) * part, cols].astype(F32)
        return total

    for t in range(0, hid, TILE):
        here, there = slice(t, t + TILE), slice(hid + t, hid + t + TILE)
        value, slope = gelu_and_slope(summed(here))
        value = value.astype(BF16)
        slope = (summed(there) * slope).astype(BF16)
        for q in range(members):
            spread[q * part : (q + 1) * part, here] = value
            spread[q * part : (q + 1) * part, there] = slope


def second_kernel(flip, zl_ref, block, up, down, up2, down2, out, rows):
    width, hid = up.shape
    part = 16
    parity = 1 - zl_ref[0] if flip else zl_ref[0]
    for q in range(rows.shape[0] // part):
        block_at = 2 * lax.rem(q + SHIFT * parity, 8) + parity
        begin = pl.multiple_of(block_at * part, part)
        rows[q * part : (q + 1) * part, :] = block[pl.ds(begin, part), :]
    out[:, :width] = matmul(rows[:, :hid], down[...], 1, 0).astype(BF16)
    out[:, width : 2 * width] = matmul(rows[:, :hid], down2[...], 1, 0).astype(BF16)
    out[:, 2 * width : 3 * width] = matmul(rows[:, hid:], up[...], 1, 1).astype(BF16)
    out[:, 3 * width :] = matmul(rows[:, hid:], up2[...], 1, 1).astype(BF16)


def pair_kernel(keep, came, out):
    out[...] = (keep[...].astype(F32) + came[...].astype(F32)).astype(BF16)


def stage_kernel(_, own, panel, first, second):
    hid = own.shape[1] // 2
    width = panel.shape[1] // 4
    first[:, :hid] = own[:, :hid]
    first[:, hid:] = panel[:, 3 * width :]
    second[:, :hid] = own[:, hid:]
    second[:, hid:] = panel[:, 2 * width : 3 * width]


def sum_kernel(parts, out):
    rows = out.shape[0]
    total = parts[:rows, :].astype(F32)
    for q in range(1, parts.shape[0] // rows):
        total = total + parts[q * rows : (q + 1) * rows, :].astype(F32)
    out[...] = total.astype(BF16)


def last_kernel(core_ref, both, output, grad_input):
    rows, width = output.shape
    part = rows // 2
    core = core_ref[0]
    for source in range(2):
        place = slice(source * part, (source + 1) * part)
        own = core == source
        output[place, :] = jnp.where(own, both[place, :width], both[place, width : 2 * width])
        grad_input[place, :] = jnp.where(
            own, both[place, 2 * width : 3 * width], both[place, 3 * width :]
        )


def grads_kernel(panel, own, first, second, grad_up, grad_down):
    width, hid = grad_up.shape
    act, cot = panel[:, :width], panel[:, width : 2 * width]
    act2, cot2 = second[:, hid:], first[:, hid:]
    for j in range(0, hid, TILE):
        cols = slice(j, j + TILE)
        grad_down[cols, :] = (
            matmul(own[:, cols], cot, 0, 0) + matmul(first[:, cols], cot2, 0, 0)
        ).astype(BF16)
        grad_up[:, cols] = (
            matmul(act, own[:, hid + j : hid + j + TILE], 0, 0)
            + matmul(act2, second[:, cols], 0, 0)
        ).astype(BF16)


def per_device(activations, up, down, cotangent):
    rows, width = activations.shape
    hid = up.shape[1]
    core = lax.axis_index("core").astype(jnp.int32).reshape(1)
    zl = (lax.axis_index("col") % 2).astype(jnp.int32).reshape(1)
    part = rows // 2
    half = 16 * part
    members = 16
    work = 8 * half * width * hid

    up2 = lax.ppermute(up, "core", SWAP)
    down2 = lax.ppermute(down, "core", SWAP)
    pair = lax.all_gather(
        jnp.concatenate([activations, cotangent], axis=1), "core", axis=0, tiled=True
    )
    (mine,) = call(pick_kernel, [shape(part, 4 * width)], 8 * work, core, zl, pair)
    panel = lax.all_gather(mine, "col", axis=0, tiled=True, axis_index_groups=[RING])

    (partial,) = call(
        first_kernel, [shape(half, 2 * hid)], work, panel, up, down, up2, down2
    )

    got = lax.all_to_all(partial, "plane", 0, 0, tiled=True, axis_index_groups=CHIPS)
    (spread,) = call(middle_kernel, [shape(half, 2 * hid)], 8 * work, got)
    own = lax.all_to_all(spread, "plane", 0, 0, tiled=True, axis_index_groups=CHIPS)

    def second(flip):
        return call(
            functools.partial(second_kernel, flip),
            [shape(half // 2, 4 * width)],
            work // 2,
            zl,
            own,
            up,
            down,
            up2,
            down2,
            scratch=[pltpu.VMEM((half // 2, 2 * hid), BF16)],
        )

    (send,) = second(True)
    came = lax.ppermute(send, "col", EVEN)
    (keep,) = second(False)
    (added,) = call(pair_kernel, [shape(half // 2, 4 * width)], 0, keep, came)
    gathered = lax.all_to_all(
        added, "col", 0, 0, tiled=True, axis_index_groups=PARITIES
    )

    pieces = call(
        stage_kernel, [shape(half, hid + width)] * 2, work // 4, added, own, panel
    )
    others = [lax.ppermute(piece, "core", SWAP) for piece in pieces]
    grad_up, grad_down = call(
        grads_kernel, [shape(width, hid), shape(hid, width)], work, panel, own, *others
    )

    gathered, grad_up, grad_down = lax.optimization_barrier((gathered, grad_up, grad_down))
    (summed,) = call(sum_kernel, [shape(part, 4 * width)], 0, gathered)
    both = lax.all_gather(summed, "core", axis=0, tiled=True)
    output, grad_input = call(last_kernel, [shape(rows, width)] * 2, 0, core, both)
    return (output, grad_input, grad_up, grad_down)


def solution(mesh):
    fine = Mesh(mesh.devices.reshape(16, 2, 16), ("plane", "core", "col"))
    row = ("plane", "core")
    return jax.shard_map(
        per_device,
        mesh=fine,
        in_specs=(P("col", row), P(row, "col"), P("col", row), P("col", row)),
        out_specs=(P("col", row), P("col", row), P(row, "col"), P("col", row)),
        check_vma=False,
    )
```

```python
import functools
import math

import jax
import jax.numpy as jnp
from jax import lax
from jax.experimental import pallas as pl
from jax.experimental.pallas import tpu as pltpu
from jax.sharding import Mesh
from jax.sharding import PartitionSpec as P

BF16 = jnp.bfloat16
F32 = jnp.float32
COEF = math.sqrt(2.0 / math.pi)
CHIPS = [list(range(15, -1, -1))]
TURN = 10
RING = [(z + TURN) % 16 for z in range(16)]
SHIFT = 5
PARITIES = [[(TURN + p * (2 * SHIFT + 1) + 2 * q) % 16 for q in range(8)] for p in range(2)]
SWAP = [(0, 1), (1, 0)]
EVEN = [(z, z ^ 1) for z in range(16)]
TILE = 256
MIB = 1024 * 1024
VMEM = pl.BlockSpec(memory_space=pltpu.VMEM)
SMEM = pl.BlockSpec(memory_space=pltpu.SMEM)


def gelu_and_slope(z):
    t = jnp.tanh(COEF * (z + 0.044715 * z * z * z))
    value = 0.5 * z * (1.0 + t)
    slope = 0.5 * (1.0 + t) + 0.5 * z * (1.0 - t * t) * COEF * (1.0 + 3.0 * 0.044715 * z * z)
    return value, slope


def matmul(a, b, left, right):
    return lax.dot_general(a, b, (((left,), (right,)), ((), ())), preferred_element_type=F32)


def call(kernel, out_shape, flops, *args, scratch=()):
    specs = [SMEM if a.dtype == jnp.int32 else VMEM for a in args]
    size = sum(a.size * a.dtype.itemsize for a in args) + sum(
        math.prod(o.shape) * o.dtype.itemsize for o in out_shape
    )
    return pl.pallas_call(
        kernel,
        out_shape=out_shape,
        in_specs=specs,
        out_specs=[VMEM] * len(out_shape),
        scratch_shapes=scratch,
        compiler_params=pltpu.CompilerParams(vmem_limit_bytes=10 * MIB),
        cost_estimate=pl.CostEstimate(flops=flops, bytes_accessed=size, transcendentals=0),
    )(*args)


def shape(*dims):
    return jax.ShapeDtypeStruct(dims, BF16)


def pick_kernel(core_ref, _, pair, out):
    part = out.shape[0]
    rows, cols = 2 * part, pair.shape[1]
    core = core_ref[0]
    mine = pl.multiple_of(core * rows + core * part, part)
    theirs = pl.multiple_of((1 - core) * rows + core * part, part)
    out[:, :cols] = pair[pl.ds(mine, part), :]
    out[:, cols:] = pair[pl.ds(theirs, part), :]


def first_kernel(panel, up, down, up2, down2, out):
    width, hid = up.shape
    act, cot, act2, cot2 = [panel[:, q * width : (q + 1) * width] for q in range(4)]
    for t in range(0, hid, TILE):
        span = slice(t, t + TILE)
        out[:, span] = (
            matmul(act, up[:, span], 1, 0) + matmul(act2, up2[:, span], 1, 0)
        ).astype(BF16)
        out[:, hid + t : hid + t + TILE] = (
            matmul(cot, down[span, :], 1, 1) + matmul(cot2, down2[span, :], 1, 1)
        ).astype(BF16)


def middle_kernel(got, spread):
    members = 16
    part = got.shape[0] // members
    hid = got.shape[1] // 2

    def summed(cols):
        total = got[:part, cols].astype(F32)
        for q in range(1, members):
            total = total + got[q * part : (q + 1) * part, cols].astype(F32)
        return total

    for t in range(0, hid, TILE):
        here, there = slice(t, t + TILE), slice(hid + t, hid + t + TILE)
        value, slope = gelu_and_slope(summed(here))
        value = value.astype(BF16)
        slope = (summed(there) * slope).astype(BF16)
        for q in range(members):
            spread[q * part : (q + 1) * part, here] = value
            spread[q * part : (q + 1) * part, there] = slope


def second_kernel(flip, zl_ref, block, up, down, up2, down2, out, rows):
    width, hid = up.shape
    part = 16
    parity = 1 - zl_ref[0] if flip else zl_ref[0]
    for q in range(rows.shape[0] // part):
        block_at = 2 * lax.rem(q + SHIFT * parity, 8) + parity
        begin = pl.multiple_of(block_at * part, part)
        rows[q * part : (q + 1) * part, :] = block[pl.ds(begin, part), :]
    out[:, :width] = matmul(rows[:, :hid], down[...], 1, 0).astype(BF16)
    out[:, width : 2 * width] = matmul(rows[:, :hid], down2[...], 1, 0).astype(BF16)
    out[:, 2 * width : 3 * width] = matmul(rows[:, hid:], up[...], 1, 1).astype(BF16)
    out[:, 3 * width :] = matmul(rows[:, hid:], up2[...], 1, 1).astype(BF16)


def pair_kernel(keep, came, out):
    out[...] = (keep[...].astype(F32) + came[...].astype(F32)).astype(BF16)


def stage_kernel(_, own, panel, first, second):
    hid = own.shape[1] // 2
    width = panel.shape[1] // 4
    first[:, :hid] = own[:, :hid]
    first[:, hid:] = panel[:, 3 * width :]
    second[:, :hid] = own[:, hid:]
    second[:, hid:] = panel[:, 2 * width : 3 * width]


def sum_kernel(parts, out):
    rows = out.shape[0]
    total = parts[:rows, :].astype(F32)
    for q in range(1, parts.shape[0] // rows):
        total = total + parts[q * rows : (q + 1) * rows, :].astype(F32)
    out[...] = total.astype(BF16)


def last_kernel(core_ref, both, output, grad_input):
    rows, width = output.shape
    part = rows // 2
    core = core_ref[0]
    for source in range(2):
        place = slice(source * part, (source + 1) * part)
        own = core == source
        output[place, :] = jnp.where(own, both[place, :width], both[place, width : 2 * width])
        grad_input[place, :] = jnp.where(
            own, both[place, 2 * width : 3 * width], both[place, 3 * width :]
        )


def grads_kernel(panel, own, first, second, grad_up, grad_down):
    width, hid = grad_up.shape
    act, cot = panel[:, :width], panel[:, width : 2 * width]
    act2, cot2 = second[:, hid:], first[:, hid:]
    for j in range(0, hid, TILE):
        cols = slice(j, j + TILE)
        grad_down[cols, :] = (
            matmul(own[:, cols], cot, 0, 0) + matmul(first[:, cols], cot2, 0, 0)
        ).astype(BF16)
        grad_up[:, cols] = (
            matmul(act, own[:, hid + j : hid + j + TILE], 0, 0)
            + matmul(act2, second[:, cols], 0, 0)
        ).astype(BF16)


def per_device(activations, up, down, cotangent):
    rows, width = activations.shape
    hid = up.shape[1]
    core = lax.axis_index("core").astype(jnp.int32).reshape(1)
    zl = (lax.axis_index("col") % 2).astype(jnp.int32).reshape(1)
    part = rows // 2
    half = 16 * part
    members = 16
    work = 8 * half * width * hid

    up2 = lax.ppermute(up, "core", SWAP)
    down2 = lax.ppermute(down, "core", SWAP)
    pair = lax.all_gather(
        jnp.concatenate([activations, cotangent], axis=1), "core", axis=0, tiled=True
    )
    (mine,) = call(pick_kernel, [shape(part, 4 * width)], 8 * work, core, zl, pair)
    panel = lax.all_gather(mine, "col", axis=0, tiled=True, axis_index_groups=[RING])

    (partial,) = call(
        first_kernel, [shape(half, 2 * hid)], work, panel, up, down, up2, down2
    )

    got = lax.all_to_all(partial, "plane", 0, 0, tiled=True, axis_index_groups=CHIPS)
    (spread,) = call(middle_kernel, [shape(half, 2 * hid)], 8 * work, got)
    own = lax.all_to_all(spread, "plane", 0, 0, tiled=True, axis_index_groups=CHIPS)

    def second(flip):
        return call(
            functools.partial(second_kernel, flip),
            [shape(half // 2, 4 * width)],
            work // 2,
            zl,
            own,
            up,
            down,
            up2,
            down2,
            scratch=[pltpu.VMEM((half // 2, 2 * hid), BF16)],
        )

    (send,) = second(True)
    came = lax.ppermute(send, "col", EVEN)
    (keep,) = second(False)
    (added,) = call(pair_kernel, [shape(half // 2, 4 * width)], 0, keep, came)
    gathered = lax.all_to_all(
        added, "col", 0, 0, tiled=True, axis_index_groups=PARITIES
    )

    pieces = call(
        stage_kernel, [shape(half, hid + width)] * 2, work // 4, added, own, panel
    )
    others = [lax.ppermute(piece, "core", SWAP) for piece in pieces]
    grad_up, grad_down = call(
        grads_kernel, [shape(width, hid), shape(hid, width)], work, panel, own, *others
    )

    gathered, grad_up, grad_down = lax.optimization_barrier((gathered, grad_up, grad_down))
    (summed,) = call(sum_kernel, [shape(part, 4 * width)], 0, gathered)
    both = lax.all_gather(summed, "core", axis=0, tiled=True)
    output, grad_input = call(last_kernel, [shape(rows, width)] * 2, 0, core, both)
    return (output, grad_input, grad_up, grad_down)


def solution(mesh):
    fine = Mesh(mesh.devices.reshape(16, 2, 16), ("plane", "core", "col"))
    row = ("plane", "core")
    return jax.shard_map(
        per_device,
        mesh=fine,
        in_specs=(P("col", row), P(row, "col"), P("col", row), P("col", row)),
        out_specs=(P("col", row), P("col", row), P(row, "col"), P("col", row)),
        check_vma=False,
    )
```
